32 devices in a mesh: site: 4 (over y, core), sector: 8 (over z, x).
Axes of the slice: x: 2, y: 2, z: 4, core: 2. Of those that a mesh axis runs over, the one named last changes fastest.
Arguments:
- env_in: bfloat16 [64, 20, 1024], P('sector'), as said below
- mpo_terms: bfloat16 [4, 20, 20], replicated, may hold values from -1.25 to 1.25
- site_tensors: bfloat16 [4, 64, 4, 1024], P('site', 'sector'), may hold values from -0.75 to 0.75
- route_owner: int32 [4, 64, 4, 1], P('site'), may hold values from 0 to 7; in each aligned block of 32 rows (0 to 31, 32 to 63, ..., all dimensions but the last counted through in order) at most 8 rows name the same one
- route_sector: int32 [4, 64, 4], P('site'), may hold values from 0 to 7
- live_block_extent: int32 [64], P('sector'), may hold values from 8 to 32, as said below
- psi: bfloat16 [4, 64, 1024], P('site', 'sector'), may hold values from -6 to 6
- right_env: bfloat16 [4, 64, 20, 1024], P('site', 'sector'), as said below
Outputs:
- ground: float32 [4, 64, 1024], P('site', 'sector')
- site_energy: float32 [4], P('site')
The draws below stay inside these ranges and needn't reach their ends.
Inputs may be any that keep to these rules, and one draw needn't show every extreme that they name: `route_owner`: among the rows of one device at one site (8 sectors times 4 states) no owner is named more than 8 times, and some device's rows name one owner exactly 8 times. `live_block_extent`: some sector block is full in every draw. `env_in`: each block is symmetric in its two block indices for every bond index. `right_env`: each block is symmetric in its two block indices for every bond index.
All inputs are finite; a program needn't handle non-finite values.
Results may differ from the reference program's by a relative error of at most 0.03.
Values may be sent and summed in bfloat16 or wider, within the bound.
A program may use at most 64 MiB of HBM per device.

```python
import math
import jax
import jax.numpy as jnp
import numpy as np
from jax import lax

B = 32
W_BOND = 20
SEC_DEV = 8
PHYS = 4
DAV_ITERS = 2
CAP = 8
S = 64
SITES = 4
N_SECTOR = 8


def draw_env_in(key, part):
    raw_values = jax.random.normal(key, (S, W_BOND, B, B), jnp.float32)
    symmetric = (raw_values + jnp.swapaxes(raw_values, 2, 3)) * (0.7071 / math.sqrt(B))
    return symmetric.reshape(S, W_BOND, B * B).astype(jnp.bfloat16)


def draw_right_env(key, part):
    first_key, second_key = jax.random.split(jax.random.fold_in(key, 7))
    raw_values = jax.random.normal(first_key, (SITES, S, W_BOND, B, B), jnp.float32)
    diagonal = jnp.exp(jax.random.uniform(second_key, (SITES, S, B), jnp.float32, math.log(0.5), math.log(2.0)))
    symmetric = (raw_values + jnp.swapaxes(raw_values, 3, 4)) * (0.35 / math.sqrt(B * W_BOND))
    identity = jnp.eye(B, dtype=jnp.float32)
    first_bond = (jnp.arange(W_BOND) == 0).astype(jnp.float32)
    plane = first_bond[:, None, None] * identity[None, :, :]
    whole = symmetric + diagonal[:, :, None, :, None] * plane[None, None]
    return whole.reshape(SITES, S, W_BOND, B * B).astype(jnp.bfloat16)


def draw_live_block_extent(key, part):
    first_key, second_key = jax.random.split(jax.random.fold_in(key, 11))
    sizes = jax.random.randint(first_key, (S,), B // 4, B + 1)
    chosen = jax.random.randint(second_key, (), 0, S)
    return jnp.where(jnp.arange(S) == chosen, B, sizes).astype(jnp.int32)


def place_ends(entries, own_key, least, largest):
    longest = entries.shape.index(max(entries.shape))
    spots = []
    for shift in (0, 1):
        where = [jax.random.randint(jax.random.fold_in(own_key, axis), (), 0, length) for axis, length in enumerate(entries.shape)]
        where[longest] = (where[longest] + shift) % entries.shape[longest]
        spots.append(tuple(where))
    return entries.at[spots[0]].set(least).at[spots[1]].set(largest)


def steps_of(stream_key, dims, pieces, low, high):
    def one(position, blocks):
        steps = jax.random.uniform(jax.random.fold_in(jax.random.fold_in(stream_key, 6), position), (blocks,), jnp.float32, low / len(pieces), high / len(pieces))
        return jnp.repeat(jnp.exp(steps), dims[position] // blocks).reshape((-1,) + (1,) * (len(dims) - position - 1))

    gain = one(*pieces[0])
    for cut in pieces[1:]:
        gain = gain * one(*cut)
    return gain


def shared_out(own_key, own, number, rows, number_of, top, most, skew):
    sequence = jax.random.permutation(own_key, number_of)
    crowded, ordinary = load_shares(number_of, rows * top, most, skew, True), load_shares(number_of, rows * top, most, skew, False)
    places = jnp.arange(number_of)

    def named(sizes, offset_by):
        used = int((sizes > 0).sum())
        fixed = max(1, used // 4)
        shifted = fixed + (places - fixed + offset_by * (used - fixed)) % max(1, number_of - fixed)
        return jnp.zeros((number_of,), jnp.int32).at[sequence[jnp.where(places < fixed, places, shifted)]].set(jnp.asarray(sizes, jnp.int32))

    sizes = jnp.where(number % 4 == 0, named(crowded, number // 4), named(ordinary, number - number // 4 - 1))
    mixed = jax.random.permutation(jax.random.fold_in(own, 3), number_of)
    source_of, sink = mixed[0:number_of // 2 * 2:2], mixed[1:number_of // 2 * 2:2]
    margin = jnp.minimum(sizes[source_of] - 1, most - sizes[sink]) // 2
    margin = jnp.where((source_of == sequence[0]) | (sink == sequence[0]) | (sizes[sink] == 0), 0, jnp.maximum(margin, 0))
    shifted = jax.random.randint(jax.random.fold_in(own, 4), (number_of // 2,), 0, 1 << 20) % (margin + 1)
    sizes = sizes.at[source_of].add(-shifted).at[sink].add(shifted)
    labels = jnp.searchsorted(jnp.cumsum(sizes), jnp.arange(rows * top), side="right").astype(jnp.int32)
    listing = labels.reshape(top, rows).T
    listing = listing[jax.random.permutation(jax.random.fold_in(own, 1), rows)]
    offset_by = jax.random.randint(jax.random.fold_in(own, 2), (rows, 1), 0, top)
    return jnp.take_along_axis(listing, (jnp.arange(top)[None, :] + offset_by) % top, axis=1)


def load_shares(amount, total, reach, slope, full):
    loads = [(1 << 20) // math.isqrt(grade ** slope) + 1 for grade in range(1, amount + 1)]
    largest = reach if full else min(reach, max(-(-total // amount), total * loads[0] // sum(loads)))
    least = 1 if total - largest >= amount - 1 else 0
    given, spare = [largest] + [least] * (amount - 1), total - largest - least * (amount - 1)
    while spare > 0:
        movable = [i for i in range(1, amount) if given[i] < largest] or [i for i in range(1, amount) if given[i] < reach]
        whole, budget = sum([loads[i] for i in movable]), spare
        for i in movable:
            extra = min(reach - given[i], max(1, budget * loads[i] // whole), spare)
            given[i] = given[i] + extra
            spare = spare - extra
    return np.array(given)


def centred(stream_key, shape, width, reach, pieces=(), kind=jnp.bfloat16):
    drawn = jax.random.normal(stream_key, shape, jnp.float32) * width
    if len(pieces) > 0:
        drawn = steps_of(stream_key, shape, pieces, -0.22, 0.18) * drawn
    return jnp.clip(drawn, min=-reach, max=reach).astype(kind)


def setup_inputs(seed: int = 0) -> dict:
    key_of = jax.random.split(jax.random.key(seed), 9)
    env_in = draw_env_in(jax.random.fold_in(key_of[8], 71), 0)
    mpo_terms = centred(key_of[1], (PHYS, W_BOND, W_BOND), W_BOND ** -0.5, 1.25)
    site_tensors = centred(key_of[2], (SITES, S, PHYS, B * B), (2 * B) ** -0.5, 0.75, ((0, 4), (1, 8)))
    route_owner_keys = jax.random.split(jax.random.fold_in(key_of[3], 1), SITES * S * PHYS // (SEC_DEV * PHYS))
    route_owner_turns = jax.random.permutation(jax.random.fold_in(key_of[3], 3), SITES * S * PHYS // (SEC_DEV * PHYS))
    route_owner = jax.vmap(lambda own, number: shared_out(jax.random.fold_in(key_of[3], 2), own, number, SEC_DEV * PHYS, N_SECTOR, 1, CAP, 2))(route_owner_keys, route_owner_turns).reshape((SITES, S, PHYS, 1))
    route_sector = place_ends(jax.random.randint(key_of[4], (SITES, S, PHYS), 0, SEC_DEV), jax.random.fold_in(key_of[4], 1), 0, SEC_DEV - 1).astype(jnp.int32)
    live_block_extent = draw_live_block_extent(jax.random.fold_in(key_of[8], 71), 0)
    psi = centred(key_of[6], (SITES, S, B * B), 1.0, 6.0, ((0, 4), (1, 8)))
    right_env = draw_right_env(jax.random.fold_in(key_of[8], 71), 0)
    return dict(env_in=env_in, mpo_terms=mpo_terms, site_tensors=site_tensors, route_owner=route_owner, route_sector=route_sector, live_block_extent=live_block_extent, psi=psi, right_env=right_env)


epsilon = 1e-06

def spread(values):
    return values[:, None, None, None]

def reference(env_in, mpo_terms, site_tensors, route_owner, route_sector, live_block_extent, psi, right_env):
    count_all = S * B * B
    target = (route_owner[..., 0] * SEC_DEV + route_sector).astype(jnp.int32)
    mpo_full = mpo_terms.astype(jnp.float32)

    def chain_step(left_env, inputs):
        tensors, goals = inputs
        env_blocks = left_env.reshape(S, W_BOND, B, B).astype(jnp.float32)
        tensor_blocks = tensors.reshape(S, PHYS, B, B).astype(jnp.float32)
        mixed = jnp.einsum('swab,pwv->spvab', env_blocks, mpo_full).astype(jnp.bfloat16)
        halfway = jnp.einsum('spvab,spbc->spvac', mixed.astype(jnp.float32), tensor_blocks).astype(jnp.bfloat16)
        blocks = jnp.einsum('spad,spvac->spvdc', tensor_blocks, halfway.astype(jnp.float32)).astype(jnp.bfloat16)
        summed = jax.ops.segment_sum(blocks.astype(jnp.float32).reshape(S * PHYS, W_BOND, B * B), goals.reshape(S * PHYS), num_segments=S)
        return (summed.astype(jnp.bfloat16), left_env)
    last_env, left_environments = lax.scan(chain_step, env_in, (site_tensors, target))
    site_positions = jnp.arange(B, dtype=jnp.int32)
    live_flags = site_positions[None, :] < live_block_extent[:, None]
    sector_block_mask = (live_flags[:, :, None] & live_flags[:, None, :]).astype(jnp.float32)
    left_full = left_environments.astype(jnp.float32).reshape(SITES, S, W_BOND, B, B)
    right_full = right_env.astype(jnp.float32).reshape(SITES, S, W_BOND, B, B)

    def operate(field):
        product = jnp.einsum('nswab,nsbc->nswac', left_full, field, precision=lax.Precision.HIGHEST)
        product = jnp.einsum('nswac,nswcd->nsad', product, right_full, precision=lax.Precision.HIGHEST)
        return product * sector_block_mask

    def inner_product(former, latter):
        return lax.optimization_barrier(jnp.sum(former * latter, axis=(1, 2, 3))) / count_all
    left_diag = jnp.diagonal(left_full, axis1=3, axis2=4)
    right_diag = jnp.diagonal(right_full, axis1=3, axis2=4)
    precond = jnp.einsum('nswa,nswb->nsab', left_diag, right_diag, precision=lax.Precision.HIGHEST)
    start = psi.astype(jnp.float32).reshape(SITES, S, B, B) * sector_block_mask
    trial_vector = start / spread(jnp.sqrt(inner_product(start, start) + epsilon))
    image = operate(trial_vector)
    energy = inner_product(trial_vector, image)
    for sweep_index in range(DAV_ITERS):
        residual_vector = image - spread(energy) * trial_vector
        correction = residual_vector / jnp.maximum(precond - spread(energy), 1.0)
        correlation = inner_product(trial_vector, correction)
        orthogonal = correction - spread(correlation) * trial_vector
        direction = orthogonal / spread(jnp.sqrt(inner_product(orthogonal, orthogonal) + epsilon))
        applied = operate(direction)
        coupling = inner_product(direction, image)
        curvature = inner_product(direction, applied)
        angle = 0.5 * jnp.arctan2(-2.0 * coupling, curvature - energy)
        trial_vector = spread(jnp.cos(angle)) * trial_vector + spread(jnp.sin(angle)) * direction
        image = spread(jnp.cos(angle)) * image + spread(jnp.sin(angle)) * applied
        energy = inner_product(trial_vector, image)
    return (trial_vector.reshape(SITES, S, B * B), energy)
```

```python
import functools

import jax
import jax.numpy as jnp
from jax import lax
from jax.experimental import pallas as pl
from jax.experimental.pallas import tpu as pltpu
from jax.sharding import PartitionSpec as P

B = 32
DAV_ITERS = 2
MESH = pl.DeviceIdType.MESH
F32 = jnp.float32
BF16 = jnp.bfloat16

epsilon = 1e-06


def iota(shape, axis):
    return lax.broadcasted_iota(jnp.int32, shape, axis)


def ones_where(condition, kind=BF16):
    return jnp.where(condition, 1.0, 0.0).astype(F32).astype(kind)


def dot(left, right):
    return jnp.dot(left, right, preferred_element_type=F32)


def kernel(
    n_site, n_sector, sec, phys, bond, count_all,
    env_ref, mpo_ref, msg_ref, start_ref, mask_ref, right_ref,
    ground_ref, energy_ref,
    mix, tbuf, part, rsbuf, ebuf, ecur, lbuf, zbuf, blocks, redbuf, redout, diag_right, qbuf,
    t_send, t_recv, rs_send, rs_recv, ag_send, ag_recv, red_send, red_recv,
):
    site = lax.axis_index("site")
    member = lax.axis_index("sector")
    rows_a = sec * B
    wide = bond * B
    chunks = wide // 128
    dr = B // n_site
    own = sec * dr
    cols = phys * own
    t_rows = rows_a
    last = n_site - 1

    def site_peer(k):
        return lax.rem(site + k, n_site)

    def sector_peer(k):
        return lax.rem(member + k, n_sector)

    barrier = pltpu.get_barrier_semaphore()
    for k in range(1, n_site):
        pl.semaphore_signal(barrier, inc=1, device_id=(site_peer(k), member), device_id_type=MESH)
    for k in range(1, n_sector):
        pl.semaphore_signal(barrier, inc=1, device_id=(site, sector_peer(k)), device_id_type=MESH)
    pl.semaphore_wait(barrier, n_site + n_sector - 2)

    def t_copy(k, source):
        return pltpu.make_async_remote_copy(
            src_ref=msg_ref, dst_ref=tbuf.at[source], send_sem=t_send.at[k], recv_sem=t_recv.at[source],
            device_id=(site_peer(k), member), device_id_type=MESH,
        )

    @pl.when(site < last)
    def _():
        for k in range(1, n_site):
            t_copy(k, site).start()

    tbuf[site] = msg_ref[...]

    spread_rows = ones_where(iota((wide, bond), 0) // B == iota((wide, bond), 1))
    spread_cols = ones_where(iota((bond, wide), 1) // B == iota((bond, wide), 0))
    eye_wide = ones_where(iota((wide, wide), 0) % B == iota((wide, wide), 1) % B)
    for p in range(phys):
        tall = dot(spread_rows, mpo_ref[p]).astype(BF16)
        mix[p] = dot(tall, spread_cols).astype(BF16) * eye_wide

    row, col = iota((rows_a, rows_a), 0), iota((rows_a, rows_a), 1)
    source = (row % B) // dr * own + row // B * dr + row % dr
    permute = ones_where(col == source)
    row, col = iota((cols, phys * B), 0), iota((cols, phys * B), 1)
    pick_rows = ones_where((row // own == col // B) & (col % B == site * dr + row % dr))
    row, col = iota((cols, rows_a), 0), iota((cols, rows_a), 1)
    same_sector = ones_where((row % own) // dr == col // B)
    row, col = iota((phys * B, phys * 128), 0), iota((phys * B, phys * 128), 1)
    repeat4 = ones_where((row // B == col // 128) & (row % B == col % B))
    row, col = iota((128, phys * 128), 0), iota((128, phys * 128), 1)
    block4 = ones_where(row // B == (col % 128) // B)

    lanes_r = sec * B
    row, col = iota((wide, lanes_r), 0), iota((wide, lanes_r), 1)
    masked_right = right_ref[...] * ones_where(row % B == col % B)
    folded = dot(spread_cols, masked_right).astype(BF16)
    diag_right[...] = dot(spread_rows, folded).astype(BF16)

    ecur[...] = env_ref[...]

    @pl.when(site == 0)
    def _():
        lbuf[...] = env_ref[...]

    def rs_copy(step, k, source):
        peer = sector_peer(k)
        return pltpu.make_async_remote_copy(
            src_ref=part.at[step, pl.ds(pl.multiple_of(peer * own, own), own)],
            dst_ref=rsbuf.at[step, source],
            send_sem=rs_send.at[step, k], recv_sem=rs_recv.at[step, source],
            device_id=(site, peer), device_id_type=MESH,
        )

    def ag_copy(step, k, source):
        rows = pl.ds(pl.multiple_of(source * own, own), own)
        return pltpu.make_async_remote_copy(
            src_ref=ebuf.at[step, rows], dst_ref=ebuf.at[step, rows],
            send_sem=ag_send.at[step, k], recv_sem=ag_recv.at[step, source],
            device_id=(site_peer(k), member), device_id_type=MESH,
        )

    def chain_step(step, carry):
        @pl.when(step != site)
        def _():
            t_copy(1, step).wait_recv()

        tensors = tbuf[step, pl.ds(0, t_rows)]
        goals = tbuf[step, pl.ds(t_rows, 16)].astype(F32)
        repeated = dot(tensors, repeat4).astype(BF16)
        for s in range(sec):
            rows = pl.ds(s * B, B)
            piece = repeated[s * B:(s + 1) * B]
            weights = jnp.concatenate([piece] * 4, axis=0) * block4
            stacked = jnp.concatenate([ecur[rows, pl.ds(j * 128, 128)] for j in range(chunks)], axis=0)
            product = dot(stacked, weights).astype(BF16)
            for p in range(phys):
                for j in range(chunks):
                    zbuf[p, rows, pl.ds(j * 128, 128)] = product[j * B:(j + 1) * B, p * 128:(p + 1) * 128]
        left = lax.dot_general(pick_rows, tensors, (((1,), (1,)), ((), ())), preferred_element_type=F32)
        left = left.astype(BF16) * same_sector
        for p in range(phys):
            half = dot(left[p * own:(p + 1) * own], zbuf[p]).astype(BF16)
            blocks[pl.ds(p * own, own)] = dot(half, mix[p]).astype(BF16)
        goal_row = jnp.concatenate([goals[r:r + 1] for r in range(cols // 128)], axis=1)
        rows_all = n_sector * own
        row, col = iota((rows_all, cols), 0), iota((rows_all, cols), 1)
        wanted = jnp.where(row % dr == col % dr, (row // dr).astype(F32), -1.0)
        routing = ones_where(wanted == goal_row)
        part[step] = dot(routing, blocks[...]).astype(BF16)
        for k in range(1, n_sector):
            rs_copy(step, k, member).start()
        total = part[step, pl.ds(pl.multiple_of(member * own, own), own)].astype(F32)
        for k in range(1, n_sector):
            source = sector_peer(k)
            rs_copy(step, k, source).wait_recv()
            total = total + rsbuf[step, source].astype(F32)
        ebuf[step, pl.ds(pl.multiple_of(site * own, own), own)] = total.astype(BF16)
        for k in range(1, n_site):
            @pl.when((step < last - 1) | (site_peer(k) == last))
            def _():
                ag_copy(step, k, site).start()

        @pl.when((step < last - 1) | (site == last))
        def _():
            for k in range(1, n_site):
                ag_copy(step, k, site_peer(k)).wait_recv()
            ecur[...] = dot(permute, ebuf[step]).astype(BF16)

        @pl.when(step + 1 == site)
        def _():
            lbuf[...] = ecur[...]

        return carry

    lax.fori_loop(0, last, chain_step, 0)

    live = mask_ref[...]
    field = (rows_a, 128)
    row, col = iota((rows_a, lanes_r), 0), iota((rows_a, lanes_r), 1)
    own_lanes = ones_where(row // B == col // B, F32)
    row, col = iota((128, 128), 0), iota((128, 128), 1)
    same4 = ones_where(row // B == col // B)
    row, col = iota((rows_a, wide), 0), iota((rows_a, wide), 1)
    left_diag = lbuf[...] * ones_where(row % B == col % B)

    def own_sector(values):
        values = values * own_lanes
        folded = values[:, 0:128]
        for j in range(1, lanes_r // 128):
            folded = folded + values[:, j * 128:(j + 1) * 128]
        folded = folded + pltpu.roll(folded, 32, 1)
        return folded + pltpu.roll(folded, 64, 1)

    precond = own_sector(dot(left_diag, diag_right[...]))

    def operate(x):
        high = x.astype(BF16)
        low = (x - high.astype(F32)).astype(BF16)
        for s in range(sec):
            rows = pl.ds(s * B, B)
            weights = jnp.concatenate(
                [
                    jnp.concatenate([part_x[s * B:(s + 1) * B]] * 4, axis=0) * same4
                    for part_x in (high, low)
                ],
                axis=1,
            )
            stacked = jnp.concatenate([lbuf[rows, pl.ds(j * 128, 128)] for j in range(chunks)], axis=0)
            product = dot(stacked, weights)
            product = product[:, 0:128] + product[:, 128:256]
            for j in range(chunks):
                qbuf[rows, pl.ds(j * 128, 128)] = product[j * B:(j + 1) * B]
        middle = qbuf[...]
        high = middle.astype(BF16)
        low = (middle - high.astype(F32)).astype(BF16)
        return own_sector(dot(high, right_ref[...]) + dot(low, right_ref[...])) * live

    def red_copy(turn, k, source):
        return pltpu.make_async_remote_copy(
            src_ref=redout.at[turn], dst_ref=redbuf.at[turn, source],
            send_sem=red_send.at[turn, k], recv_sem=red_recv.at[turn, source],
            device_id=(site, sector_peer(k)), device_id_type=MESH,
        )

    def reduce(turn, pairs):
        sums = [jnp.sum(x * y, axis=0, keepdims=True) for x, y in pairs]
        sums = sums + [jnp.zeros((1, 128), F32)] * (8 - len(sums))
        redout[turn] = jnp.concatenate(sums, axis=0)
        for k in range(1, n_sector):
            red_copy(turn, k, member).start()
        redbuf[turn, member] = redout[turn]
        for k in range(1, n_sector):
            red_copy(turn, k, sector_peer(k)).wait_recv()
        total = redbuf[turn, 0]
        for j in range(1, n_sector):
            total = total + redbuf[turn, j]
        total = jnp.sum(total, axis=1, keepdims=True) * (0.25 / count_all)
        return [total[j:j + 1] for j in range(len(pairs))]

    start = start_ref[...]
    image = operate(start)
    norm, energy = reduce(0, [(start, start), (start, image)])
    scale = 1.0 / jnp.sqrt(norm + epsilon)
    vector = start * scale
    image = image * scale
    energy = energy * scale * scale
    for turn in range(1, DAV_ITERS + 1):
        correction = (image - energy * vector) / jnp.maximum(precond - energy, 1.0)
        applied = operate(correction)
        vc, cc, vv, ci, ca, va, vi = reduce(
            turn,
            [
                (vector, correction), (correction, correction), (vector, vector), (correction, image),
                (correction, applied), (vector, applied), (vector, image),
            ],
        )
        length_sq = jnp.maximum(cc - 2.0 * vc * vc + vc * vc * vv, 0.0)
        scale = 1.0 / jnp.sqrt(length_sq + epsilon)
        direction = (correction - vc * vector) * scale
        applied = (applied - vc * image) * scale
        coupling = (ci - vc * vi) * scale
        curvature = (ca - vc * ci - vc * va + vc * vc * vi) * scale * scale
        crossing = (va - vc * vi) * scale
        y, x = -2.0 * coupling, curvature - energy
        largest = jnp.maximum(jnp.abs(x), jnp.abs(y))
        safe = jnp.where(largest > 0.0, largest, 1.0)
        x, y = jnp.where(largest > 0.0, x / safe, 1.0), y / safe
        radius = jnp.sqrt(x * x + y * y)
        big = jnp.sqrt((radius + jnp.abs(x)) / (2.0 * radius))
        small = jnp.abs(y) / (2.0 * radius * big)
        cosine = jnp.where(x >= 0.0, big, small)
        sine = jnp.where(x >= 0.0, small, big) * jnp.where(y > 0.0, 1.0, -1.0)
        energy = cosine * cosine * vi + cosine * sine * (crossing + coupling) + sine * sine * curvature
        vector = cosine * vector + sine * direction
        image = cosine * image + sine * applied
    ground_ref[...] = vector
    energy_ref[...] = jnp.broadcast_to(energy, (8, 128))

    @pl.when(site < last)
    def _():
        for k in range(1, n_site):
            t_copy(k, site).wait_send()

    def sent(step, carry):
        for k in range(1, n_sector):
            rs_copy(step, k, member).wait_send()
        for k in range(1, n_site):
            @pl.when((step < last - 1) | (site_peer(k) == last))
            def _():
                ag_copy(step, k, site).wait_send()
        return carry

    lax.fori_loop(0, last, sent, 0)
    for turn in range(DAV_ITERS + 1):
        for k in range(1, n_sector):
            red_copy(turn, k, member).wait_send()


def local(
    env_in, mpo_terms, site_tensors, route_owner, route_sector, live_block_extent, psi, right_env
):
    n_sector = lax.axis_size("sector")
    n_site = lax.axis_size("site")
    member = lax.axis_index("sector")
    sec, bond = env_in.shape[0], env_in.shape[1]
    phys = site_tensors.shape[2]
    steps = n_site - 1
    dr = B // n_site
    own = sec * dr
    cols = phys * own
    rows_a, wide = sec * B, bond * B

    env = env_in.reshape(sec, bond, B, B).transpose(0, 2, 1, 3).reshape(rows_a, wide)
    right = right_env.reshape(sec, bond, B, B).transpose(1, 2, 0, 3).reshape(wide, rows_a)
    tensors = site_tensors.reshape(sec, phys, B, B).transpose(0, 2, 1, 3).reshape(rows_a, phys * B)
    target = route_owner[0, :, :, 0] * sec + route_sector[0]
    target = lax.dynamic_slice_in_dim(target, member * sec, sec, 0)
    goals = jnp.broadcast_to(target.T[:, :, None], (phys, sec, dr)).reshape(cols // 128, 128)
    goals = jnp.pad(goals.astype(BF16), ((0, 16 - cols // 128), (0, 0)))
    message = jnp.concatenate([tensors, goals], axis=0)
    index = jnp.arange(B, dtype=jnp.int32)
    flags = index[None, :] < live_block_extent[:, None]
    live = (flags[:, :, None] & flags[:, None, :]).astype(F32)
    start = psi.astype(F32).reshape(sec, B, B) * live
    live = jnp.tile(live.reshape(rows_a, B), (1, 4))
    start = jnp.tile(start.reshape(rows_a, B), (1, 4))

    count_all = float(sec * n_sector * B * B)
    dma = pltpu.SemaphoreType.DMA
    ground, energy = pl.pallas_call(
        functools.partial(kernel, n_site, n_sector, sec, phys, bond, count_all),
        out_shape=(
            jax.ShapeDtypeStruct((rows_a, 128), F32),
            jax.ShapeDtypeStruct((8, 128), F32),
        ),
        in_specs=[pl.BlockSpec(memory_space=pltpu.VMEM)] * 6,
        out_specs=[pl.BlockSpec(memory_space=pltpu.VMEM)] * 2,
        scratch_shapes=[
            pltpu.VMEM((phys, wide, wide), BF16),
            pltpu.VMEM((n_site, rows_a + 16, 128), BF16),
            pltpu.VMEM((steps, n_sector * own, wide), BF16),
            pltpu.VMEM((steps, n_sector, own, wide), BF16),
            pltpu.VMEM((steps, rows_a, wide), BF16),
            pltpu.VMEM((rows_a, wide), BF16),
            pltpu.VMEM((rows_a, wide), BF16),
            pltpu.VMEM((phys, rows_a, wide), BF16),
            pltpu.VMEM((cols, wide), BF16),
            pltpu.VMEM((DAV_ITERS + 1, n_sector, 8, 128), F32),
            pltpu.VMEM((DAV_ITERS + 1, 8, 128), F32),
            pltpu.VMEM((wide, rows_a), BF16),
            pltpu.VMEM((rows_a, wide), F32),
            dma((n_site,)), dma((n_site,)),
            dma((steps, n_sector)), dma((steps, n_sector)),
            dma((steps, n_site)), dma((steps, n_site)),
            dma((DAV_ITERS + 1, n_sector)), dma((DAV_ITERS + 1, n_sector)),
        ],
        compiler_params=pltpu.CompilerParams(
            collective_id=0, has_side_effects=True, vmem_limit_bytes=50 * 1024 * 1024
        ),
    )(env, mpo_terms, message, start, live, right)
    return ground[:, :B].reshape(1, sec, B * B), energy[0, :1]


def solution(mesh):
    in_specs = (
        P("sector", None, None),
        P(),
        P("site", "sector", None, None),
        P("site", None, None, None),
        P("site", None, None),
        P("sector"),
        P("site", "sector", None),
        P("site", "sector", None, None),
    )
    out_specs = (P("site", "sector", None), P("site"))
    return jax.shard_map(local, mesh=mesh, in_specs=in_specs, out_specs=out_specs, check_vma=False)
```

```python
import functools

import jax
import jax.numpy as jnp
from jax import lax
from jax.experimental import pallas as pl
from jax.experimental.pallas import tpu as pltpu
from jax.sharding import PartitionSpec as P

B = 32
DAV_ITERS = 2
MESH = pl.DeviceIdType.MESH
F32 = jnp.float32
BF16 = jnp.bfloat16

epsilon = 1e-06


def iota(shape, axis):
    return lax.broadcasted_iota(jnp.int32, shape, axis)


def flag(condition, kind=BF16):
    return jnp.where(condition, 1.0, 0.0).astype(F32).astype(kind)


def dot(left, right):
    return jnp.dot(left, right, preferred_element_type=F32)


def dot_rows(left, right):
    return lax.dot_general(left, right, (((1,), (1,)), ((), ())), preferred_element_type=F32)


def kernel(
    n_site, n_sector, sec, phys, bond, count_all, parts,
    env_ref, right_ref, tensor_ref, psi_ref, mpo_ref, goals_ref, extent_ref,
    ground_ref, energy_ref,
    mix, tbuf, part, xbuf, sbuf, rsbuf, ebuf, ecur, lbuf, zbuf, blocks, wbuf, leftbuf, routing,
    redbuf, redout, right_t, diag_right, qbuf, stage,
    t_send, t_recv, x_send, x_recv, rs_send, rs_recv, ag_send, ag_recv, red_send, red_recv,
):
    site = lax.axis_index("site")
    member = lax.axis_index("sector")
    n_low = 2
    n_high = n_sector // n_low
    high = member // n_low
    low = member % n_low
    rows_a = sec * B
    wide = bond * B
    chunks = wide // 128
    dr = B // n_site
    own = sec * dr
    cols = phys * own
    last = n_site - 1
    group = iota((B, 128), 0) & 3
    in_group = iota((B, 128), 1) >> 5 == group
    upper = iota((8, 128), 0) < 4
    takes = [[((group + turn) & 3 == k) & in_group for k in range(4)] for turn in range(4)]

    def unpack(rows):
        spread = [
            jnp.concatenate(
                [
                    jnp.where(
                        upper,
                        jnp.broadcast_to(stage[pl.ds(r, 1), pl.ds(256 * q, 128)], (8, 128)),
                        jnp.broadcast_to(stage[pl.ds(r, 1), pl.ds(256 * q + 128, 128)], (8, 128)),
                    )
                    for q in range(4)
                ],
                axis=0,
            )
            for r in rows
        ]
        whole = None
        for turn in range(4):
            moved = jnp.where(takes[turn][0], spread[0], 0.0)
            for k in range(1, 4):
                moved = jnp.where(takes[turn][k], spread[k], moved)
            whole = moved if turn == 0 else whole + pltpu.roll(moved, 32 * turn, 1)
        return whole

    def unpack_bonds(source, target):
        def one(s, carry):
            stage[pl.ds(0, bond)] = source[s].astype(F32)
            rows = pl.ds(pl.multiple_of(s * B, B), B)
            for j in range(chunks):
                target[rows, pl.ds(j * 128, 128)] = unpack(range(4 * j, 4 * j + 4)).astype(target.dtype)
            return carry

        lax.fori_loop(0, sec, one, 0)

    def site_peer(k):
        return lax.rem(site + k, n_site)

    def sector_peer(k):
        return lax.rem(member + k, n_sector)

    def high_peer(k):
        return lax.rem(high + k, n_high)

    barrier = pltpu.get_barrier_semaphore()
    for k in range(1, n_site):
        pl.semaphore_signal(barrier, inc=1, device_id=(site_peer(k), member), device_id_type=MESH)
    for k in range(1, n_sector):
        pl.semaphore_signal(barrier, inc=1, device_id=(site, sector_peer(k)), device_id_type=MESH)
    for s in range(sec):
        stage[pl.ds(0, phys)] = tensor_ref[s].astype(F32)
        tbuf[site, pl.ds(s * B, B)] = unpack(range(phys)).astype(BF16)
    tbuf[site, pl.ds(rows_a, 16)] = goals_ref[...]
    pl.semaphore_wait(barrier, n_site + n_sector - 2)

    def t_copy(k, source):
        return pltpu.make_async_remote_copy(
            src_ref=tbuf.at[source], dst_ref=tbuf.at[source],
            send_sem=t_send.at[k], recv_sem=t_recv.at[source],
            device_id=(site_peer(k), member), device_id_type=MESH,
        )

    def t_start():
        for k in range(1, n_site):
            t_copy(k, site).start()

    pl.when(site == 0)(t_start)

    spread_rows = flag(iota((wide, bond), 0) >> 5 == iota((wide, bond), 1))
    spread_cols = flag(iota((bond, wide), 1) >> 5 == iota((bond, wide), 0))
    eye_wide = flag((iota((wide, wide), 0) - iota((wide, wide), 1)) & 31 == 0)
    for p in range(phys):
        tall = dot(spread_rows, mpo_ref[p]).astype(BF16)
        mix[p] = dot(tall, spread_cols).astype(BF16) * eye_wide

    row, col = iota((rows_a, rows_a), 0), iota((rows_a, rows_a), 1)
    permute = flag(col == (row % B) // dr * own + row // B * dr + row % dr)
    row, col = iota((cols, phys * B), 0), iota((cols, phys * B), 1)
    pick_rows = flag((row // own == col // B) & (col % B == site * dr + row % dr))
    row, col = iota((cols, rows_a), 0), iota((cols, rows_a), 1)
    same_sector = flag((row % own) // dr == col // B)
    row, col = iota((phys * B, phys * 128), 0), iota((phys * B, phys * 128), 1)
    repeat4 = flag((row >> 5 == col >> 7) & (row & 31 == col & 31))
    row, col = iota((128, phys * 128), 0), iota((128, phys * 128), 1)
    block4 = flag(row >> 5 == (col & 127) >> 5)

    @pl.when((site > 0) & (site < last))
    def _():
        t_start()

    def prepare(step):
        @pl.when(step != site)
        def _():
            t_copy(1, step).wait_recv()

        tensors = tbuf[step, pl.ds(0, rows_a)]
        goals = tbuf[step, pl.ds(rows_a, 16)].astype(F32)
        repeated = dot(tensors, repeat4).astype(BF16)
        for s in range(sec):
            piece = repeated[s * B:(s + 1) * B]
            wbuf[s] = jnp.concatenate([piece] * 4, axis=0) * block4
        leftbuf[...] = dot_rows(pick_rows, tensors).astype(BF16) * same_sector
        goal_row = jnp.concatenate([goals[r:r + 1] for r in range(cols // 128)], axis=1)
        rows_all = n_sector * own
        row, col = iota((rows_all, cols), 0), iota((rows_all, cols), 1)
        wanted = jnp.where((row - col) & (dr - 1) == 0, (row // dr).astype(F32), -1.0)
        routing[...] = flag(wanted == goal_row)

    def prepare_right():
        unpack_bonds(right_ref, qbuf)
        right_t[...] = qbuf[...].T.astype(BF16)

    def right_diagonal():
        row, col = iota((wide, rows_a), 0), iota((wide, rows_a), 1)
        masked = right_t[...] * flag((row - col) & 31 == 0)
        folded = dot(spread_cols, masked).astype(BF16)
        diag_right[...] = dot(spread_rows, folded).astype(BF16)

    unpack_bonds(env_ref, ecur)
    prepare(0)

    @pl.when(site == 0)
    def _():
        lbuf[...] = ecur[...]

    def chunk_rows(high_of, low_of):
        return pl.ds(pl.multiple_of((high_of * n_low + low_of) * own, own), own)

    def x_copy(step, c, k):
        lanes = pl.ds(*parts[c])
        block = high_peer(k)
        return pltpu.make_async_remote_copy(
            src_ref=part.at[step, chunk_rows(block, 1 - low), lanes],
            dst_ref=xbuf.at[step, k, :, lanes],
            send_sem=x_send.at[step, c, k], recv_sem=x_recv.at[step, c, k],
            device_id=(site, high * n_low + 1 - low), device_id_type=MESH,
        )

    def rs_copy(step, c, k, source):
        lanes = pl.ds(*parts[c])
        return pltpu.make_async_remote_copy(
            src_ref=sbuf.at[step, k, :, lanes],
            dst_ref=rsbuf.at[step, source, :, lanes],
            send_sem=rs_send.at[step, c, k], recv_sem=rs_recv.at[step, c, source],
            device_id=(site, high_peer(k) * n_low + low), device_id_type=MESH,
        )

    def ag_copy(step, c, k, source):
        lanes = pl.ds(*parts[c])
        rows = pl.ds(pl.multiple_of(source * own, own), own)
        return pltpu.make_async_remote_copy(
            src_ref=ebuf.at[step, rows, lanes], dst_ref=ebuf.at[step, rows, lanes],
            send_sem=ag_send.at[step, c, k], recv_sem=ag_recv.at[step, c, source],
            device_id=(site_peer(k), member), device_id_type=MESH,
        )

    n_parts = len(parts)
    order = list(range(1, n_high)) + [0]

    def chain_step(step, carry):
        for s in range(sec):
            rows = pl.ds(s * B, B)
            stacked = jnp.concatenate([ecur[rows, pl.ds(j * 128, 128)] for j in range(chunks)], axis=0)
            product = dot(stacked, wbuf[s]).astype(BF16)
            for p in range(phys):
                for j in range(chunks):
                    zbuf[p, rows, pl.ds(j * 128, 128)] = product[j * B:(j + 1) * B, p * 128:(p + 1) * 128]
        for p in range(phys):
            half = dot(leftbuf[pl.ds(p * own, own)], zbuf[p]).astype(BF16)
            blocks[pl.ds(p * own, own)] = dot(half, mix[p]).astype(BF16)
        for k in order:
            rows = pl.ds(pl.multiple_of(high_peer(k) * n_low * own, n_low * own), n_low * own)
            part[step, rows] = dot(routing[rows], blocks[...]).astype(BF16)
            x_copy(step, 0, k).start()
        for c in range(1, n_parts):
            for k in order:
                x_copy(step, c, k).start()

        @pl.when(step + 1 < last)
        def _():
            prepare(step + 1)

        pl.when(step == 0)(prepare_right)
        pl.when(step + 1 == last)(right_diagonal)

        totals = []
        for c in range(n_parts):
            lanes = pl.ds(*parts[c])
            for k in order:
                x_copy(step, c, k).wait_recv()
                mine = part[step, chunk_rows(high_peer(k), low), lanes].astype(F32)
                mine = mine + xbuf[step, k, :, lanes].astype(F32)
                if k == 0:
                    totals.append(mine)
                else:
                    sbuf[step, k, :, lanes] = mine.astype(BF16)
                    rs_copy(step, c, k, high).start()
        for c in range(n_parts):
            lanes = pl.ds(*parts[c])
            total = totals[c]
            for k in range(1, n_high):
                source = high_peer(k)
                rs_copy(step, c, k, source).wait_recv()
                total = total + rsbuf[step, source, :, lanes].astype(F32)
            ebuf[step, pl.ds(pl.multiple_of(site * own, own), own), lanes] = total.astype(BF16)
            for k in range(1, n_site):
                @pl.when((step < last - 1) | (site_peer(k) == last))
                def _():
                    ag_copy(step, c, k, site).start()

        @pl.when((step < last - 1) | (site == last))
        def _():
            for c in range(n_parts):
                lanes = pl.ds(*parts[c])
                for k in range(1, n_site):
                    ag_copy(step, c, k, site_peer(k)).wait_recv()
                ecur[:, lanes] = dot(permute, ebuf[step, :, lanes]).astype(BF16)

        @pl.when(step + 1 == site)
        def _():
            lbuf[...] = ecur[...]

        return carry

    lax.fori_loop(0, last, chain_step, 0)

    row, col = iota((rows_a, 128), 0), iota((rows_a, 128), 1)
    extent = extent_ref[...]
    live = flag(((row & 31).astype(F32) < extent) & ((col & 31).astype(F32) < extent), F32)
    row, col = iota((rows_a, rows_a), 0), iota((rows_a, rows_a), 1)
    own_lanes = flag(row >> 5 == col >> 5, F32)
    row, col = iota((128, 128), 0), iota((128, 128), 1)
    same4 = flag(row >> 5 == col >> 5)
    row, col = iota((rows_a, wide), 0), iota((rows_a, wide), 1)
    left_diag = lbuf[...] * flag((row - col) & 31 == 0)

    def four_copies(values):
        values = values + pltpu.roll(values, 32, 1)
        return values + pltpu.roll(values, 64, 1)

    def own_sector(values):
        values = values * own_lanes
        folded = values[:, 0:128]
        for j in range(1, rows_a // 128):
            folded = folded + values[:, j * 128:(j + 1) * 128]
        return four_copies(folded)

    def operate(x):
        x = x.astype(BF16)
        for s in range(sec):
            rows = pl.ds(s * B, B)
            weights = jnp.concatenate([x[s * B:(s + 1) * B]] * 4, axis=0) * same4
            stacked = jnp.concatenate([lbuf[rows, pl.ds(j * 128, 128)] for j in range(chunks)], axis=0)
            product = dot(stacked, weights).astype(BF16)
            for j in range(chunks):
                ecur[rows, pl.ds(j * 128, 128)] = product[j * B:(j + 1) * B]
        return own_sector(dot(ecur[...], right_t[...])) * live

    def red_copy(turn, k, source):
        return pltpu.make_async_remote_copy(
            src_ref=redout.at[turn], dst_ref=redbuf.at[turn, source],
            send_sem=red_send.at[turn, k], recv_sem=red_recv.at[turn, source],
            device_id=(site, sector_peer(k)), device_id_type=MESH,
        )

    def reduce(turn, pairs, meanwhile=None):
        sums = [jnp.sum(x * y, axis=0, keepdims=True) for x, y in pairs]
        sums = sums + [jnp.zeros((1, 128), F32)] * (8 - len(sums))
        redout[turn] = jnp.concatenate(sums, axis=0)
        for k in range(1, n_sector):
            red_copy(turn, k, member).start()
        redbuf[turn, member] = redout[turn]
        made = meanwhile() if meanwhile else None
        for k in range(1, n_sector):
            red_copy(turn, k, sector_peer(k)).wait_recv()
        total = redbuf[turn, 0]
        for j in range(1, n_sector):
            total = total + redbuf[turn, j]
        total = jnp.sum(total, axis=1, keepdims=True) * (0.25 / count_all)
        return [total[j:j + 1] for j in range(len(pairs))], made

    stage[pl.ds(0, sec)] = psi_ref[...].astype(F32)
    start = jnp.concatenate([unpack([s] * 4) for s in range(sec)], axis=0) * live
    image = operate(start)
    (norm, energy), precond = reduce(
        0, [(start, start), (start, image)], lambda: own_sector(dot(left_diag, diag_right[...]))
    )
    scale = 1.0 / jnp.sqrt(norm + epsilon)
    vector = start * scale
    image = image * scale
    energy = energy * scale * scale
    for turn in range(1, DAV_ITERS + 1):
        correction = (image - energy * vector) / jnp.maximum(precond - energy, 1.0)
        applied = operate(correction)
        (vc, cc, vv, ci, ca, va, vi), _ = reduce(
            turn,
            [
                (vector, correction), (correction, correction), (vector, vector), (correction, image),
                (correction, applied), (vector, applied), (vector, image),
            ],
        )
        length_sq = jnp.maximum(cc - 2.0 * vc * vc + vc * vc * vv, 0.0)
        scale = 1.0 / jnp.sqrt(length_sq + epsilon)
        direction = (correction - vc * vector) * scale
        applied = (applied - vc * image) * scale
        coupling = (ci - vc * vi) * scale
        curvature = (ca - vc * ci - vc * va + vc * vc * vi) * scale * scale
        crossing = (va - vc * vi) * scale
        y, x = -2.0 * coupling, curvature - energy
        largest = jnp.maximum(jnp.abs(x), jnp.abs(y))
        safe = jnp.where(largest > 0.0, largest, 1.0)
        x, y = jnp.where(largest > 0.0, x / safe, 1.0), y / safe
        radius = jnp.sqrt(x * x + y * y)
        big = jnp.sqrt((radius + jnp.abs(x)) / (2.0 * radius))
        small = jnp.abs(y) / (2.0 * radius * big)
        cosine = jnp.where(x >= 0.0, big, small)
        sine = jnp.where(x >= 0.0, small, big) * jnp.where(y > 0.0, 1.0, -1.0)
        energy = cosine * cosine * vi + cosine * sine * (crossing + coupling) + sine * sine * curvature
        vector = cosine * vector + sine * direction
        image = cosine * image + sine * applied
    row, col = iota((rows_a, 128), 0), iota((rows_a, 128), 1)
    for j in range(B * B // 128):
        kept = jnp.where((row & 31) == (col >> 5) + 4 * j, vector, 0.0)
        ground_ref[:, pl.ds(j * 128, 128)] = jnp.sum(kept.reshape(sec, B, 128), axis=1)
    energy_ref[...] = jnp.broadcast_to(energy, (8, 128))

    @pl.when(site < last)
    def _():
        for k in range(1, n_site):
            t_copy(k, site).wait_send()

    def sent(step, carry):
        for c in range(n_parts):
            for k in range(n_high):
                x_copy(step, c, k).wait_send()
                if k > 0:
                    rs_copy(step, c, k, high).wait_send()
            for k in range(1, n_site):
                @pl.when((step < last - 1) | (site_peer(k) == last))
                def _():
                    ag_copy(step, c, k, site).wait_send()
        return carry

    lax.fori_loop(0, last, sent, 0)
    for turn in range(DAV_ITERS + 1):
        for k in range(1, n_sector):
            red_copy(turn, k, member).wait_send()


def local(
    env_in, mpo_terms, site_tensors, route_owner, route_sector, live_block_extent, psi, right_env
):
    n_sector = lax.axis_size("sector")
    n_site = lax.axis_size("site")
    member = lax.axis_index("sector")
    sec, bond = env_in.shape[0], env_in.shape[1]
    phys = site_tensors.shape[2]
    steps = n_site - 1
    n_high = n_sector // 2
    dr = B // n_site
    own = sec * dr
    cols = phys * own
    rows_a, wide = sec * B, bond * B
    cut = (wide // 128 + 1) // 2 * 128
    parts = ((0, cut), (cut, wide - cut))

    target = route_owner[0, :, :, 0] * sec + route_sector[0]
    target = lax.dynamic_slice_in_dim(target, member * sec, sec, 0)
    goals = jnp.broadcast_to(target.T[:, :, None], (phys, sec, dr)).reshape(cols // 128, 128)
    goals = jnp.pad(goals.astype(BF16), ((0, 16 - cols // 128), (0, 0)))
    extent = jnp.broadcast_to(live_block_extent.astype(F32)[:, None, None], (sec, B, 128)).reshape(rows_a, 128)

    count_all = float(sec * n_sector * B * B)
    dma = pltpu.SemaphoreType.DMA
    ground, energy = pl.pallas_call(
        functools.partial(kernel, n_site, n_sector, sec, phys, bond, count_all, parts),
        out_shape=(
            jax.ShapeDtypeStruct((sec, B * B), F32),
            jax.ShapeDtypeStruct((8, 128), F32),
        ),
        in_specs=[pl.BlockSpec(memory_space=pltpu.VMEM)] * 7,
        out_specs=[pl.BlockSpec(memory_space=pltpu.VMEM)] * 2,
        scratch_shapes=[
            pltpu.VMEM((phys, wide, wide), BF16),
            pltpu.VMEM((n_site, rows_a + 16, 128), BF16),
            pltpu.VMEM((steps, n_sector * own, wide), BF16),
            pltpu.VMEM((steps, n_high, own, wide), BF16),
            pltpu.VMEM((steps, n_high, own, wide), BF16),
            pltpu.VMEM((steps, n_high, own, wide), BF16),
            pltpu.VMEM((steps, rows_a, wide), BF16),
            pltpu.VMEM((rows_a, wide), BF16),
            pltpu.VMEM((rows_a, wide), BF16),
            pltpu.VMEM((phys, rows_a, wide), BF16),
            pltpu.VMEM((cols, wide), BF16),
            pltpu.VMEM((sec, 128, phys * 128), BF16),
            pltpu.VMEM((cols, rows_a), BF16),
            pltpu.VMEM((n_sector * own, cols), BF16),
            pltpu.VMEM((DAV_ITERS + 1, n_sector, 8, 128), F32),
            pltpu.VMEM((DAV_ITERS + 1, 8, 128), F32),
            pltpu.VMEM((wide, rows_a), BF16),
            pltpu.VMEM((wide, rows_a), BF16),
            pltpu.VMEM((rows_a, wide), F32),
            pltpu.VMEM((max(bond, sec) + 4, B * B), F32),
            dma((n_site,)), dma((n_site,)),
            dma((steps, 2, n_high)), dma((steps, 2, n_high)),
            dma((steps, 2, n_high)), dma((steps, 2, n_high)),
            dma((steps, 2, n_site)), dma((steps, 2, n_site)),
            dma((DAV_ITERS + 1, n_sector)), dma((DAV_ITERS + 1, n_sector)),
        ],
        compiler_params=pltpu.CompilerParams(
            collective_id=0, has_side_effects=True, vmem_limit_bytes=50 * 1024 * 1024
        ),
    )(env_in, right_env[0], site_tensors[0], psi[0], mpo_terms, goals, extent)
    return ground[None], energy[0, :1]


def solution(mesh):
    in_specs = (
        P("sector", None, None),
        P(),
        P("site", "sector", None, None),
        P("site", None, None, None),
        P("site", None, None),
        P("sector"),
        P("site", "sector", None),
        P("site", "sector", None, None),
    )
    out_specs = (P("site", "sector", None), P("site"))
    return jax.shard_map(local, mesh=mesh, in_specs=in_specs, out_specs=out_specs, check_vma=False)
```

```python
import functools

import jax
import jax.numpy as jnp
from jax import lax
from jax.experimental import pallas as pl
from jax.experimental.pallas import tpu as pltpu
from jax.sharding import PartitionSpec as P

B = 32
DAV_ITERS = 2
MESH = pl.DeviceIdType.MESH
F32 = jnp.float32
BF16 = jnp.bfloat16

epsilon = 1e-06


def iota(shape, axis):
    return lax.broadcasted_iota(jnp.int32, shape, axis)


def flag(condition, kind=BF16):
    return jnp.where(condition, 1.0, 0.0).astype(F32).astype(kind)


def dot(left, right):
    return jnp.dot(left, right, preferred_element_type=F32)


def dot_rows(left, right):
    return lax.dot_general(left, right, (((1,), (1,)), ((), ())), preferred_element_type=F32)


def kernel(
    n_site, n_sector, sec, phys, bond, count_all, parts,
    env_ref, right_ref, tensor_ref, psi_ref, mpo_ref, goals_ref, extent_ref,
    ground_ref, energy_ref,
    mix, tbuf, part, xbuf, sbuf, rsbuf, ebuf, ecur, lbuf, zbuf, halves, wbuf, leftbuf, routing,
    redbuf, redout, right_t, diag_right, qbuf, stage, env_in, right_in,
    t_send, t_recv, x_send, x_recv, rs_send, rs_recv, ag_send, ag_recv, red_send, red_recv, fetch_sem,
):
    site = lax.axis_index("site")
    member = lax.axis_index("sector")
    n_low = 2
    n_high = n_sector // n_low
    high = member // n_low
    low = member % n_low
    rows_a = sec * B
    wide = bond * B
    chunks = wide // 128
    dr = B // n_site
    own = sec * dr
    cols = phys * own
    last = n_site - 1
    group = iota((B, 128), 0) & 3
    in_group = iota((B, 128), 1) >> 5 == group
    upper = iota((8, 128), 0) < 4
    takes = [[((group + turn) & 3 == k) & in_group for k in range(4)] for turn in range(4)]

    def unpack(pieces):
        spread = [
            jnp.concatenate(
                [
                    jnp.where(
                        upper,
                        jnp.broadcast_to(piece(pl.ds(256 * q, 128)), (8, 128)),
                        jnp.broadcast_to(piece(pl.ds(256 * q + 128, 128)), (8, 128)),
                    )
                    for q in range(4)
                ],
                axis=0,
            )
            for piece in pieces
        ]
        whole = None
        for turn in range(4):
            moved = jnp.where(takes[turn][0], spread[0], 0.0)
            for k in range(1, 4):
                moved = jnp.where(takes[turn][k], spread[k], moved)
            whole = moved if turn == 0 else whole + pltpu.roll(moved, 32 * turn, 1)
        return whole

    def unpack_bonds(source, target):
        stage[...] = source[...].astype(F32)

        def one(j, carry):
            lanes_out = pl.ds(pl.multiple_of(j * 128, 128), 128)
            for s in range(sec):
                pieces = [lambda lanes, k=k: stage[4 * j + k, pl.ds(s, 1), lanes] for k in range(4)]
                target[pl.ds(s * B, B), lanes_out] = unpack(pieces).astype(target.dtype)
            return carry

        lax.fori_loop(0, chunks, one, 0)

    def site_peer(k):
        return lax.rem(site + k, n_site)

    def sector_peer(k):
        return lax.rem(member + k, n_sector)

    def high_peer(k):
        return lax.rem(high + k, n_high)

    def fetch_env():
        return pltpu.make_async_copy(env_ref, env_in, fetch_sem.at[0])

    def fetch_right():
        return pltpu.make_async_copy(right_ref, right_in, fetch_sem.at[1])

    fetch_env().start()
    fetch_right().start()
    barrier = pltpu.get_barrier_semaphore()
    for k in range(1, n_site):
        pl.semaphore_signal(barrier, inc=1, device_id=(site_peer(k), member), device_id_type=MESH)
    for k in range(1, n_sector):
        pl.semaphore_signal(barrier, inc=1, device_id=(site, sector_peer(k)), device_id_type=MESH)
    for s in range(sec):
        stage[0, pl.ds(0, phys)] = tensor_ref[s].astype(F32)
        pieces = [lambda lanes, p=p: stage[0, pl.ds(p, 1), lanes] for p in range(phys)]
        tbuf[site, pl.ds(s * B, B)] = unpack(pieces).astype(BF16)
    tbuf[site, pl.ds(rows_a, 16)] = goals_ref[...]
    pl.semaphore_wait(barrier, n_site + n_sector - 2)

    def t_copy(k, source):
        return pltpu.make_async_remote_copy(
            src_ref=tbuf.at[source], dst_ref=tbuf.at[source],
            send_sem=t_send.at[k], recv_sem=t_recv.at[source],
            device_id=(site_peer(k), member), device_id_type=MESH,
        )

    def t_start():
        for k in range(1, n_site):
            t_copy(k, site).start()

    pl.when(site == 0)(t_start)


    spread_rows = flag(iota((wide, bond), 0) >> 5 == iota((wide, bond), 1))
    spread_cols = flag(iota((bond, wide), 1) >> 5 == iota((bond, wide), 0))
    eye_wide = flag((iota((wide, wide), 0) - iota((wide, wide), 1)) & 31 == 0)
    for p in range(phys):
        tall = dot(spread_rows, mpo_ref[p]).astype(BF16)
        mix[p] = dot(tall, spread_cols).astype(BF16) * eye_wide

    row, col = iota((rows_a, rows_a), 0), iota((rows_a, rows_a), 1)
    permute = flag(col == (row % B) // dr * own + row // B * dr + row % dr)
    row, col = iota((cols, phys * B), 0), iota((cols, phys * B), 1)
    pick_rows = flag((row // own == col // B) & (col % B == site * dr + row % dr))
    row, col = iota((cols, rows_a), 0), iota((cols, rows_a), 1)
    same_sector = flag((row % own) // dr == col // B)
    row, col = iota((phys * B, phys * 128), 0), iota((phys * B, phys * 128), 1)
    repeat4 = flag((row >> 5 == col >> 7) & (row & 31 == col & 31))
    row, col = iota((128, phys * 128), 0), iota((128, phys * 128), 1)
    block4 = flag(row >> 5 == (col & 127) >> 5)

    @pl.when((site > 0) & (site < last))
    def _():
        t_start()

    def prepare(step):
        @pl.when(step != site)
        def _():
            t_copy(1, step).wait_recv()

        tensors = tbuf[step, pl.ds(0, rows_a)]
        goals = tbuf[step, pl.ds(rows_a, 16)].astype(F32)
        repeated = dot(tensors, repeat4).astype(BF16)
        for s in range(sec):
            piece = repeated[s * B:(s + 1) * B]
            wbuf[s] = jnp.concatenate([piece] * 4, axis=0) * block4
        leftbuf[...] = dot_rows(pick_rows, tensors).astype(BF16) * same_sector
        goal_row = jnp.concatenate([goals[r:r + 1] for r in range(cols // 128)], axis=1)
        rows_all = n_sector * own
        row, col = iota((rows_all, cols), 0), iota((rows_all, cols), 1)
        wanted = jnp.where((row - col) & (dr - 1) == 0, (row // dr).astype(F32), -1.0)
        routing[...] = flag(wanted == goal_row)

    def prepare_right():
        fetch_right().wait()
        unpack_bonds(right_in, qbuf)
        right_t[...] = qbuf[...].T.astype(BF16)

    def right_diagonal():
        row, col = iota((wide, rows_a), 0), iota((wide, rows_a), 1)
        masked = right_t[...] * flag((row - col) & 31 == 0)
        folded = dot(spread_cols, masked).astype(BF16)
        diag_right[...] = dot(spread_rows, folded).astype(BF16)

    fetch_env().wait()
    unpack_bonds(env_in, ecur)
    prepare(0)

    @pl.when(site == 0)
    def _():
        lbuf[...] = ecur[...]

    def chunk_rows(high_of, low_of):
        return pl.ds(pl.multiple_of((high_of * n_low + low_of) * own, own), own)

    def x_copy(step, c, k):
        lanes = pl.ds(*parts[c])
        block = high_peer(k)
        return pltpu.make_async_remote_copy(
            src_ref=part.at[step, chunk_rows(block, 1 - low), lanes],
            dst_ref=xbuf.at[step, k, :, lanes],
            send_sem=x_send.at[step, c, k], recv_sem=x_recv.at[step, c, k],
            device_id=(site, high * n_low + 1 - low), device_id_type=MESH,
        )

    def rs_copy(step, c, k, source):
        lanes = pl.ds(*parts[c])
        return pltpu.make_async_remote_copy(
            src_ref=sbuf.at[step, k, :, lanes],
            dst_ref=rsbuf.at[step, source, :, lanes],
            send_sem=rs_send.at[step, c, k], recv_sem=rs_recv.at[step, c, source],
            device_id=(site, high_peer(k) * n_low + low), device_id_type=MESH,
        )

    def ag_copy(step, c, k, source):
        lanes = pl.ds(*parts[c])
        rows = pl.ds(pl.multiple_of(source * own, own), own)
        return pltpu.make_async_remote_copy(
            src_ref=ebuf.at[step, rows, lanes], dst_ref=ebuf.at[step, rows, lanes],
            send_sem=ag_send.at[step, c, k], recv_sem=ag_recv.at[step, c, source],
            device_id=(site_peer(k), member), device_id_type=MESH,
        )

    n_parts = len(parts)
    order = list(range(1, n_high)) + [0]

    def chain_step(step, carry):
        for s in range(sec):
            rows = pl.ds(s * B, B)
            stacked = jnp.concatenate([ecur[rows, pl.ds(j * 128, 128)] for j in range(chunks)], axis=0)
            product = dot(stacked, wbuf[s]).astype(BF16)
            for p in range(phys):
                for j in range(chunks):
                    zbuf[p, rows, pl.ds(j * 128, 128)] = product[j * B:(j + 1) * B, p * 128:(p + 1) * 128]
        for p in range(phys):
            halves[pl.ds(p * own, own)] = dot(leftbuf[pl.ds(p * own, own)], zbuf[p]).astype(BF16)
        for c in range(n_parts):
            lanes = pl.ds(*parts[c])
            made = jnp.concatenate(
                [dot(halves[pl.ds(p * own, own)], mix[p, :, lanes]).astype(BF16) for p in range(phys)], axis=0
            )
            for k in order:
                rows = pl.ds(pl.multiple_of(high_peer(k) * n_low * own, n_low * own), n_low * own)
                part[step, rows, lanes] = dot(routing[rows], made).astype(BF16)
                x_copy(step, c, k).start()

        @pl.when(step + 1 < last)
        def _():
            prepare(step + 1)

        pl.when(step == 0)(prepare_right)
        pl.when(step + 1 == last)(right_diagonal)

        totals = []
        for c in range(n_parts):
            lanes = pl.ds(*parts[c])
            for k in order:
                x_copy(step, c, k).wait_recv()
                mine = part[step, chunk_rows(high_peer(k), low), lanes].astype(F32)
                mine = mine + xbuf[step, k, :, lanes].astype(F32)
                if k == 0:
                    totals.append(mine)
                else:
                    sbuf[step, k, :, lanes] = mine.astype(BF16)
                    rs_copy(step, c, k, high).start()
        for c in range(n_parts):
            lanes = pl.ds(*parts[c])
            total = totals[c]
            for k in range(1, n_high):
                source = high_peer(k)
                rs_copy(step, c, k, source).wait_recv()
                total = total + rsbuf[step, source, :, lanes].astype(F32)
            ebuf[step, pl.ds(pl.multiple_of(site * own, own), own), lanes] = total.astype(BF16)
            for k in range(1, n_site):
                @pl.when((step < last - 1) | (site_peer(k) == last))
                def _():
                    ag_copy(step, c, k, site).start()

        @pl.when((step < last - 1) | (site == last))
        def _():
            for c in range(n_parts):
                lanes = pl.ds(*parts[c])
                for k in range(1, n_site):
                    ag_copy(step, c, k, site_peer(k)).wait_recv()
                ecur[:, lanes] = dot(permute, ebuf[step, :, lanes]).astype(BF16)

        @pl.when(step + 1 == site)
        def _():
            lbuf[...] = ecur[...]

        return carry

    lax.fori_loop(0, last, chain_step, 0)

    row, col = iota((rows_a, 128), 0), iota((rows_a, 128), 1)
    extent = extent_ref[...]
    live = flag(((row & 31).astype(F32) < extent) & ((col & 31).astype(F32) < extent), F32)
    row, col = iota((rows_a, rows_a), 0), iota((rows_a, rows_a), 1)
    own_lanes = flag(row >> 5 == col >> 5, F32)
    row, col = iota((128, 128), 0), iota((128, 128), 1)
    same4 = flag(row >> 5 == col >> 5)
    row, col = iota((rows_a, wide), 0), iota((rows_a, wide), 1)
    left_diag = lbuf[...] * flag((row - col) & 31 == 0)

    def four_copies(values):
        values = values + pltpu.roll(values, 32, 1)
        return values + pltpu.roll(values, 64, 1)

    def own_sector(values):
        values = values * own_lanes
        folded = values[:, 0:128]
        for j in range(1, rows_a // 128):
            folded = folded + values[:, j * 128:(j + 1) * 128]
        return four_copies(folded)

    def operate(x):
        x = x.astype(BF16)
        for s in range(sec):
            rows = pl.ds(s * B, B)
            weights = jnp.concatenate([x[s * B:(s + 1) * B]] * 4, axis=0) * same4
            stacked = jnp.concatenate([lbuf[rows, pl.ds(j * 128, 128)] for j in range(chunks)], axis=0)
            product = dot(stacked, weights).astype(BF16)
            for j in range(chunks):
                ecur[rows, pl.ds(j * 128, 128)] = product[j * B:(j + 1) * B]
        return own_sector(dot(ecur[...], right_t[...])) * live

    def red_copy(turn, k, source):
        return pltpu.make_async_remote_copy(
            src_ref=redout.at[turn], dst_ref=redbuf.at[turn, source],
            send_sem=red_send.at[turn, k], recv_sem=red_recv.at[turn, source],
            device_id=(site, sector_peer(k)), device_id_type=MESH,
        )

    def reduce(turn, pairs, meanwhile=None):
        sums = [jnp.sum(x * y, axis=0, keepdims=True) for x, y in pairs]
        sums = sums + [jnp.zeros((1, 128), F32)] * (8 - len(sums))
        redout[turn] = jnp.concatenate(sums, axis=0)
        for k in range(1, n_sector):
            red_copy(turn, k, member).start()
        redbuf[turn, member] = redout[turn]
        made = meanwhile() if meanwhile else None
        for k in range(1, n_sector):
            red_copy(turn, k, sector_peer(k)).wait_recv()
        total = redbuf[turn, 0]
        for j in range(1, n_sector):
            total = total + redbuf[turn, j]
        total = jnp.sum(total, axis=1, keepdims=True) * (0.25 / count_all)
        return [total[j:j + 1] for j in range(len(pairs))], made

    stage[0] = psi_ref[...].astype(F32)
    start = jnp.concatenate(
        [unpack([lambda lanes, s=s: stage[0, pl.ds(s, 1), lanes]] * 4) for s in range(sec)], axis=0
    ) * live
    image = operate(start)
    (norm, energy), precond = reduce(
        0, [(start, start), (start, image)], lambda: own_sector(dot(left_diag, diag_right[...]))
    )
    scale = 1.0 / jnp.sqrt(norm + epsilon)
    vector = start * scale
    image = image * scale
    energy = energy * scale * scale
    for turn in range(1, DAV_ITERS + 1):
        correction = (image - energy * vector) / jnp.maximum(precond - energy, 1.0)
        applied = operate(correction)
        (vc, cc, vv, ci, ca, va, vi), _ = reduce(
            turn,
            [
                (vector, correction), (correction, correction), (vector, vector), (correction, image),
                (correction, applied), (vector, applied), (vector, image),
            ],
        )
        length_sq = jnp.maximum(cc - 2.0 * vc * vc + vc * vc * vv, 0.0)
        scale = 1.0 / jnp.sqrt(length_sq + epsilon)
        direction = (correction - vc * vector) * scale
        applied = (applied - vc * image) * scale
        coupling = (ci - vc * vi) * scale
        curvature = (ca - vc * ci - vc * va + vc * vc * vi) * scale * scale
        crossing = (va - vc * vi) * scale
        y, x = -2.0 * coupling, curvature - energy
        largest = jnp.maximum(jnp.abs(x), jnp.abs(y))
        safe = jnp.where(largest > 0.0, largest, 1.0)
        x, y = jnp.where(largest > 0.0, x / safe, 1.0), y / safe
        radius = jnp.sqrt(x * x + y * y)
        big = jnp.sqrt((radius + jnp.abs(x)) / (2.0 * radius))
        small = jnp.abs(y) / (2.0 * radius * big)
        cosine = jnp.where(x >= 0.0, big, small)
        sine = jnp.where(x >= 0.0, small, big) * jnp.where(y > 0.0, 1.0, -1.0)
        energy = cosine * cosine * vi + cosine * sine * (crossing + coupling) + sine * sine * curvature
        vector = cosine * vector + sine * direction
        image = cosine * image + sine * applied
    row, col = iota((rows_a, 128), 0), iota((rows_a, 128), 1)
    for j in range(B * B // 128):
        kept = jnp.where((row & 31) == (col >> 5) + 4 * j, vector, 0.0)
        ground_ref[:, pl.ds(j * 128, 128)] = jnp.sum(kept.reshape(sec, B, 128), axis=1)
    energy_ref[0] = energy[0, 0]

    @pl.when(site < last)
    def _():
        for k in range(1, n_site):
            t_copy(k, site).wait_send()

    def sent(step, carry):
        for c in range(n_parts):
            for k in range(n_high):
                x_copy(step, c, k).wait_send()
                if k > 0:
                    rs_copy(step, c, k, high).wait_send()
            for k in range(1, n_site):
                @pl.when((step < last - 1) | (site_peer(k) == last))
                def _():
                    ag_copy(step, c, k, site).wait_send()
        return carry

    lax.fori_loop(0, last, sent, 0)
    for turn in range(DAV_ITERS + 1):
        for k in range(1, n_sector):
            red_copy(turn, k, member).wait_send()


def local(
    env_in, mpo_terms, site_tensors, route_owner, route_sector, live_block_extent, psi, right_env
):
    n_sector = lax.axis_size("sector")
    n_site = lax.axis_size("site")
    member = lax.axis_index("sector")
    sec, bond = env_in.shape[0], env_in.shape[1]
    phys = site_tensors.shape[2]
    steps = n_site - 1
    n_high = n_sector // 2
    dr = B // n_site
    own = sec * dr
    cols = phys * own
    rows_a, wide = sec * B, bond * B
    parts = tuple((at, min(256, wide - at)) for at in range(0, wide, 256))
    n_parts = len(parts)

    target = route_owner[0, :, :, 0] * sec + route_sector[0]
    target = lax.dynamic_slice_in_dim(target, member * sec, sec, 0)
    goals = jnp.broadcast_to(target.T[:, :, None], (phys, sec, dr)).reshape(cols // 128, 128)
    goals = jnp.pad(goals.astype(BF16), ((0, 16 - cols // 128), (0, 0)))
    extent = jnp.broadcast_to(live_block_extent.astype(F32)[:, None, None], (sec, B, 128)).reshape(rows_a, 128)

    count_all = float(sec * n_sector * B * B)
    dma = pltpu.SemaphoreType.DMA
    ground, energy = pl.pallas_call(
        functools.partial(kernel, n_site, n_sector, sec, phys, bond, count_all, parts),
        out_shape=(
            jax.ShapeDtypeStruct((sec, B * B), F32),
            jax.ShapeDtypeStruct((1,), F32),
        ),
        in_specs=[pl.BlockSpec(memory_space=pltpu.HBM if i < 2 else pltpu.VMEM) for i in range(7)],
        out_specs=[pl.BlockSpec(memory_space=pltpu.VMEM), pl.BlockSpec(memory_space=pltpu.SMEM)],
        scratch_shapes=[
            pltpu.VMEM((phys, wide, wide), BF16),
            pltpu.VMEM((n_site, rows_a + 16, 128), BF16),
            pltpu.VMEM((steps, n_sector * own, wide), BF16),
            pltpu.VMEM((steps, n_high, own, wide), BF16),
            pltpu.VMEM((steps, n_high, own, wide), BF16),
            pltpu.VMEM((steps, n_high, own, wide), BF16),
            pltpu.VMEM((steps, rows_a, wide), BF16),
            pltpu.VMEM((rows_a, wide), BF16),
            pltpu.VMEM((rows_a, wide), BF16),
            pltpu.VMEM((phys, rows_a, wide), BF16),
            pltpu.VMEM((cols, wide), BF16),
            pltpu.VMEM((sec, 128, phys * 128), BF16),
            pltpu.VMEM((cols, rows_a), BF16),
            pltpu.VMEM((n_sector * own, cols), BF16),
            pltpu.VMEM((DAV_ITERS + 1, n_sector, 8, 128), F32),
            pltpu.VMEM((DAV_ITERS + 1, 8, 128), F32),
            pltpu.VMEM((wide, rows_a), BF16),
            pltpu.VMEM((wide, rows_a), BF16),
            pltpu.VMEM((rows_a, wide), F32),
            pltpu.VMEM((bond, sec, B * B), F32),
            pltpu.VMEM((bond, sec, B * B), BF16),
            pltpu.VMEM((bond, sec, B * B), BF16),
            dma((n_site,)), dma((n_site,)),
            dma((steps, n_parts, n_high)), dma((steps, n_parts, n_high)),
            dma((steps, n_parts, n_high)), dma((steps, n_parts, n_high)),
            dma((steps, n_parts, n_site)), dma((steps, n_parts, n_site)),
            dma((DAV_ITERS + 1, n_sector)), dma((DAV_ITERS + 1, n_sector)),
            dma((2,)),
        ],
        compiler_params=pltpu.CompilerParams(
            collective_id=0, has_side_effects=True, vmem_limit_bytes=50 * 1024 * 1024
        ),
    )(env_in.transpose(1, 0, 2), right_env[0].transpose(1, 0, 2), site_tensors[0], psi[0], mpo_terms, goals, extent)
    return ground[None], energy


def solution(mesh):
    in_specs = (
        P("sector", None, None),
        P(),
        P("site", "sector", None, None),
        P("site", None, None, None),
        P("site", None, None),
        P("sector"),
        P("site", "sector", None),
        P("site", "sector", None, None),
    )
    out_specs = (P("site", "sector", None), P("site"))
    return jax.shard_map(local, mesh=mesh, in_specs=in_specs, out_specs=out_specs, check_vma=False)
```

```python
import functools

import jax
import jax.numpy as jnp
from jax import lax
from jax.experimental import pallas as pl
from jax.experimental.pallas import tpu as pltpu
from jax.sharding import PartitionSpec as P

B = 32
DAV_ITERS = 2
MESH = pl.DeviceIdType.MESH
F32 = jnp.float32
BF16 = jnp.bfloat16

epsilon = 1e-06


def iota(shape, axis):
    return lax.broadcasted_iota(jnp.int32, shape, axis)


def flag(condition, kind=BF16):
    return jnp.where(condition, 1.0, 0.0).astype(F32).astype(kind)


def dot(left, right):
    return jnp.dot(left, right, preferred_element_type=F32)


def dot_rows(left, right):
    return lax.dot_general(left, right, (((1,), (1,)), ((), ())), preferred_element_type=F32)


def kernel(
    n_site, n_sector, sec, phys, bond, count_all, parts,
    env_ref, right_ref, tensor_ref, psi_ref, mpo_ref, goals_ref, extent_ref,
    ground_ref, energy_ref,
    mix, tbuf, part, xbuf, sbuf, rsbuf, ebuf, ecur, lbuf, zbuf, halves, wbuf, leftbuf, routing,
    redbuf, redout, right_t, diag_right, qbuf, stage, env_in, right_in,
    t_send, t_recv, x_send, x_recv, rs_send, rs_recv, ag_send, ag_recv, red_send, red_recv, fetch_sem,
):
    site = lax.axis_index("site")
    member = lax.axis_index("sector")
    n_low = 2
    n_high = n_sector // n_low
    high = member // n_low
    low = member % n_low
    rows_a = sec * B
    wide = bond * B
    chunks = wide // 128
    dr = B // n_site
    own = sec * dr
    cols = phys * own
    last = n_site - 1
    group = iota((B, 128), 0) & 3
    in_group = iota((B, 128), 1) >> 5 == group
    upper = iota((8, 128), 0) < 4
    takes = [[((group + turn) & 3 == k) & in_group for k in range(4)] for turn in range(4)]

    def unpack(pieces):
        spread = [
            jnp.concatenate(
                [
                    jnp.where(
                        upper,
                        jnp.broadcast_to(piece(pl.ds(256 * q, 128)), (8, 128)),
                        jnp.broadcast_to(piece(pl.ds(256 * q + 128, 128)), (8, 128)),
                    )
                    for q in range(4)
                ],
                axis=0,
            )
            for piece in pieces
        ]
        whole = None
        for turn in range(4):
            moved = jnp.where(takes[turn][0], spread[0], 0.0)
            for k in range(1, 4):
                moved = jnp.where(takes[turn][k], spread[k], moved)
            whole = moved if turn == 0 else whole + pltpu.roll(moved, 32 * turn, 1)
        return whole

    def unpack_bonds(source, target):
        stage[...] = source[...].astype(F32)

        def one(j, carry):
            lanes_out = pl.ds(pl.multiple_of(j * 128, 128), 128)
            for s in range(sec):
                pieces = [lambda lanes, k=k: stage[4 * j + k, pl.ds(s, 1), lanes] for k in range(4)]
                target[pl.ds(s * B, B), lanes_out] = unpack(pieces).astype(target.dtype)
            return carry

        lax.fori_loop(0, chunks, one, 0)

    def site_peer(k):
        return lax.rem(site + k, n_site)

    def sector_peer(k):
        return lax.rem(member + k, n_sector)

    def high_peer(k):
        return lax.rem(high + k, n_high)

    def fetch_env():
        return pltpu.make_async_copy(env_ref, env_in, fetch_sem.at[0])

    def fetch_right():
        return pltpu.make_async_copy(right_ref, right_in, fetch_sem.at[1])

    fetch_env().start()
    fetch_right().start()
    barrier = pltpu.get_barrier_semaphore()
    for k in range(1, n_site):
        pl.semaphore_signal(barrier, inc=1, device_id=(site_peer(k), member), device_id_type=MESH)
    for k in range(1, n_sector):
        pl.semaphore_signal(barrier, inc=1, device_id=(site, sector_peer(k)), device_id_type=MESH)
    for s in range(sec):
        stage[0, pl.ds(0, phys)] = tensor_ref[s].astype(F32)
        pieces = [lambda lanes, p=p: stage[0, pl.ds(p, 1), lanes] for p in range(phys)]
        tbuf[site, pl.ds(s * B, B)] = unpack(pieces).astype(BF16)
    tbuf[site, pl.ds(rows_a, 16)] = goals_ref[...]
    pl.semaphore_wait(barrier, n_site + n_sector - 2)

    def t_copy(k, source):
        return pltpu.make_async_remote_copy(
            src_ref=tbuf.at[source], dst_ref=tbuf.at[source],
            send_sem=t_send.at[k], recv_sem=t_recv.at[source],
            device_id=(site_peer(k), member), device_id_type=MESH,
        )

    def t_start():
        for k in range(1, n_site):
            t_copy(k, site).start()

    pl.when(site == 0)(t_start)


    spread_rows = flag(iota((wide, bond), 0) >> 5 == iota((wide, bond), 1))
    spread_cols = flag(iota((bond, wide), 1) >> 5 == iota((bond, wide), 0))
    eye_wide = flag((iota((wide, wide), 0) - iota((wide, wide), 1)) & 31 == 0)
    for p in range(phys):
        tall = dot(spread_rows, mpo_ref[p]).astype(BF16)
        mix[p] = dot(tall, spread_cols).astype(BF16) * eye_wide

    row, col = iota((rows_a, rows_a), 0), iota((rows_a, rows_a), 1)
    permute = flag(col == (row % B) // dr * own + row // B * dr + row % dr)
    row, col = iota((cols, phys * B), 0), iota((cols, phys * B), 1)
    pick_rows = flag((row // own == col // B) & (col % B == site * dr + row % dr))
    row, col = iota((cols, rows_a), 0), iota((cols, rows_a), 1)
    same_sector = flag((row % own) // dr == col // B)
    row, col = iota((phys * B, phys * 128), 0), iota((phys * B, phys * 128), 1)
    repeat4 = flag((row >> 5 == col >> 7) & (row & 31 == col & 31))
    row, col = iota((128, phys * 128), 0), iota((128, phys * 128), 1)
    block4 = flag(row >> 5 == (col & 127) >> 5)

    @pl.when((site > 0) & (site < last))
    def _():
        t_start()

    def prepare(step):
        @pl.when(step != site)
        def _():
            t_copy(1, step).wait_recv()

        tensors = tbuf[step, pl.ds(0, rows_a)]
        goals = tbuf[step, pl.ds(rows_a, 16)].astype(F32)
        repeated = dot(tensors, repeat4).astype(BF16)
        for s in range(sec):
            piece = repeated[s * B:(s + 1) * B]
            wbuf[s] = jnp.concatenate([piece] * 4, axis=0) * block4
        leftbuf[...] = dot_rows(pick_rows, tensors).astype(BF16) * same_sector
        goal_row = jnp.concatenate([goals[r:r + 1] for r in range(cols // 128)], axis=1)
        rows_all = n_sector * own
        row, col = iota((rows_all, cols), 0), iota((rows_all, cols), 1)
        wanted = jnp.where((row - col) & (dr - 1) == 0, (row // dr).astype(F32), -1.0)
        routing[...] = flag(wanted == goal_row)

    def prepare_right():
        fetch_right().wait()
        unpack_bonds(right_in, qbuf)
        right_t[...] = qbuf[...].T.astype(BF16)

    def right_diagonal():
        row, col = iota((wide, rows_a), 0), iota((wide, rows_a), 1)
        masked = right_t[...] * flag((row - col) & 31 == 0)
        folded = dot(spread_cols, masked).astype(BF16)
        diag_right[...] = dot(spread_rows, folded).astype(BF16)

    fetch_env().wait()
    unpack_bonds(env_in, ecur)
    prepare(0)

    @pl.when(site == 0)
    def _():
        lbuf[...] = ecur[...]

    def chunk_rows(high_of, low_of):
        return pl.ds(pl.multiple_of((high_of * n_low + low_of) * own, own), own)

    def x_copy(step, c, k):
        lanes = pl.ds(*parts[c])
        block = high_peer(k)
        return pltpu.make_async_remote_copy(
            src_ref=part.at[step, chunk_rows(block, 1 - low), lanes],
            dst_ref=xbuf.at[step, k, :, lanes],
            send_sem=x_send.at[step, c, k], recv_sem=x_recv.at[step, c, k],
            device_id=(site, high * n_low + 1 - low), device_id_type=MESH,
        )

    def rs_copy(step, c, k, source):
        lanes = pl.ds(*parts[c])
        return pltpu.make_async_remote_copy(
            src_ref=sbuf.at[step, k, :, lanes],
            dst_ref=rsbuf.at[step, source, :, lanes],
            send_sem=rs_send.at[step, c, k], recv_sem=rs_recv.at[step, c, source],
            device_id=(site, high_peer(k) * n_low + low), device_id_type=MESH,
        )

    def ag_copy(step, c, k, source):
        lanes = pl.ds(*parts[c])
        rows = pl.ds(pl.multiple_of(source * own, own), own)
        return pltpu.make_async_remote_copy(
            src_ref=ebuf.at[step, rows, lanes], dst_ref=ebuf.at[step, rows, lanes],
            send_sem=ag_send.at[step, c, k], recv_sem=ag_recv.at[step, c, source],
            device_id=(site_peer(k), member), device_id_type=MESH,
        )

    n_parts = len(parts)

    def tensors_sent():
        @pl.when(site < last)
        def _():
            for k in range(1, n_site):
                t_copy(k, site).wait_send()

    def sent(step):
        for c in range(n_parts):
            for k in range(n_high):
                x_copy(step, c, k).wait_send()
                if k > 0:
                    rs_copy(step, c, k, high).wait_send()
            for k in range(1, n_site):
                @pl.when((step < last - 1) | (site_peer(k) == last))
                def _():
                    ag_copy(step, c, k, site).wait_send()

    order = list(range(1, n_high)) + [0]

    def chain_step(step, carry):
        for s in range(sec):
            rows = pl.ds(s * B, B)
            stacked = jnp.concatenate([ecur[rows, pl.ds(j * 128, 128)] for j in range(chunks)], axis=0)
            product = dot(stacked, wbuf[s]).astype(BF16)
            for p in range(phys):
                for j in range(chunks):
                    zbuf[p, rows, pl.ds(j * 128, 128)] = product[j * B:(j + 1) * B, p * 128:(p + 1) * 128]
        for p in range(phys):
            halves[pl.ds(p * own, own)] = dot(leftbuf[pl.ds(p * own, own)], zbuf[p]).astype(BF16)
        for c in range(n_parts):
            lanes = pl.ds(*parts[c])
            made = jnp.concatenate(
                [dot(halves[pl.ds(p * own, own)], mix[p, :, lanes]).astype(BF16) for p in range(phys)], axis=0
            )
            for k in order:
                rows = pl.ds(pl.multiple_of(high_peer(k) * n_low * own, n_low * own), n_low * own)
                part[step, rows, lanes] = dot(routing[rows], made).astype(BF16)
                x_copy(step, c, k).start()

        @pl.when(step + 1 < last)
        def _():
            prepare(step + 1)

        pl.when(step == 0)(prepare_right)

        @pl.when(step > 0)
        def _():
            sent(step - 1)

        pl.when(step + 1 == last)(right_diagonal)

        totals = []
        for c in range(n_parts):
            lanes = pl.ds(*parts[c])
            for k in order:
                x_copy(step, c, k).wait_recv()
                mine = part[step, chunk_rows(high_peer(k), low), lanes].astype(F32)
                mine = mine + xbuf[step, k, :, lanes].astype(F32)
                if k == 0:
                    totals.append(mine)
                else:
                    sbuf[step, k, :, lanes] = mine.astype(BF16)
                    rs_copy(step, c, k, high).start()
        for c in range(n_parts):
            lanes = pl.ds(*parts[c])
            total = totals[c]
            for k in range(1, n_high):
                source = high_peer(k)
                rs_copy(step, c, k, source).wait_recv()
                total = total + rsbuf[step, source, :, lanes].astype(F32)
            ebuf[step, pl.ds(pl.multiple_of(site * own, own), own), lanes] = total.astype(BF16)
            for k in range(1, n_site):
                @pl.when((step < last - 1) | (site_peer(k) == last))
                def _():
                    ag_copy(step, c, k, site).start()

        @pl.when((step < last - 1) | (site == last))
        def _():
            for c in range(n_parts):
                lanes = pl.ds(*parts[c])
                for k in range(1, n_site):
                    ag_copy(step, c, k, site_peer(k)).wait_recv()
                ecur[:, lanes] = dot(permute, ebuf[step, :, lanes]).astype(BF16)

        @pl.when(step + 1 == site)
        def _():
            lbuf[...] = ecur[...]

        return carry

    lax.fori_loop(0, last, chain_step, 0)

    row, col = iota((rows_a, 128), 0), iota((rows_a, 128), 1)
    extent = extent_ref[...]
    live = flag(((row & 31).astype(F32) < extent) & ((col & 31).astype(F32) < extent), F32)
    row, col = iota((rows_a, rows_a), 0), iota((rows_a, rows_a), 1)
    own_lanes = flag(row >> 5 == col >> 5, F32)
    row, col = iota((128, 128), 0), iota((128, 128), 1)
    same4 = flag(row >> 5 == col >> 5)
    row, col = iota((rows_a, wide), 0), iota((rows_a, wide), 1)
    left_diag = lbuf[...] * flag((row - col) & 31 == 0)

    def four_copies(values):
        values = values + pltpu.roll(values, 32, 1)
        return values + pltpu.roll(values, 64, 1)

    def own_sector(values):
        values = values * own_lanes
        folded = values[:, 0:128]
        for j in range(1, rows_a // 128):
            folded = folded + values[:, j * 128:(j + 1) * 128]
        return four_copies(folded)

    def operate(x):
        x = x.astype(BF16)
        for s in range(sec):
            rows = pl.ds(s * B, B)
            weights = jnp.concatenate([x[s * B:(s + 1) * B]] * 4, axis=0) * same4
            stacked = jnp.concatenate([lbuf[rows, pl.ds(j * 128, 128)] for j in range(chunks)], axis=0)
            product = dot(stacked, weights).astype(BF16)
            for j in range(chunks):
                ecur[rows, pl.ds(j * 128, 128)] = product[j * B:(j + 1) * B]
        return own_sector(dot(ecur[...], right_t[...])) * live

    def red_copy(turn, k, source):
        return pltpu.make_async_remote_copy(
            src_ref=redout.at[turn], dst_ref=redbuf.at[turn, source],
            send_sem=red_send.at[turn, k], recv_sem=red_recv.at[turn, source],
            device_id=(site, sector_peer(k)), device_id_type=MESH,
        )

    def reduce(turn, pairs, meanwhile=None):
        sums = [jnp.sum(x * y, axis=0, keepdims=True) for x, y in pairs]
        sums = sums + [jnp.zeros((1, 128), F32)] * (8 - len(sums))
        redout[turn] = jnp.concatenate(sums, axis=0)
        for k in range(1, n_sector):
            red_copy(turn, k, member).start()
        redbuf[turn, member] = redout[turn]
        if turn == 0:
            tensors_sent()
            sent(last - 1)
        else:
            for k in range(1, n_sector):
                red_copy(turn - 1, k, member).wait_send()
        made = meanwhile() if meanwhile else None
        for k in range(1, n_sector):
            red_copy(turn, k, sector_peer(k)).wait_recv()
        total = redbuf[turn, 0]
        for j in range(1, n_sector):
            total = total + redbuf[turn, j]
        total = jnp.sum(total, axis=1, keepdims=True) * (0.25 / count_all)
        return [total[j:j + 1] for j in range(len(pairs))], made

    stage[0] = psi_ref[...].astype(F32)
    start = jnp.concatenate(
        [unpack([lambda lanes, s=s: stage[0, pl.ds(s, 1), lanes]] * 4) for s in range(sec)], axis=0
    ) * live
    image = operate(start)
    (norm, energy), precond = reduce(
        0, [(start, start), (start, image)], lambda: own_sector(dot(left_diag, diag_right[...]))
    )
    scale = 1.0 / jnp.sqrt(norm + epsilon)
    vector = start * scale
    image = image * scale
    energy = energy * scale * scale
    for turn in range(1, DAV_ITERS + 1):
        correction = (image - energy * vector) / jnp.maximum(precond - energy, 1.0)
        applied = operate(correction)
        (vc, cc, vv, ci, ca, va, vi), _ = reduce(
            turn,
            [
                (vector, correction), (correction, correction), (vector, vector), (correction, image),
                (correction, applied), (vector, applied), (vector, image),
            ],
        )
        length_sq = jnp.maximum(cc - 2.0 * vc * vc + vc * vc * vv, 0.0)
        scale = 1.0 / jnp.sqrt(length_sq + epsilon)
        direction = (correction - vc * vector) * scale
        applied = (applied - vc * image) * scale
        coupling = (ci - vc * vi) * scale
        curvature = (ca - vc * ci - vc * va + vc * vc * vi) * scale * scale
        crossing = (va - vc * vi) * scale
        y, x = -2.0 * coupling, curvature - energy
        largest = jnp.maximum(jnp.abs(x), jnp.abs(y))
        safe = jnp.where(largest > 0.0, largest, 1.0)
        x, y = jnp.where(largest > 0.0, x / safe, 1.0), y / safe
        radius = jnp.sqrt(x * x + y * y)
        big = jnp.sqrt((radius + jnp.abs(x)) / (2.0 * radius))
        small = jnp.abs(y) / (2.0 * radius * big)
        cosine = jnp.where(x >= 0.0, big, small)
        sine = jnp.where(x >= 0.0, small, big) * jnp.where(y > 0.0, 1.0, -1.0)
        energy = cosine * cosine * vi + cosine * sine * (crossing + coupling) + sine * sine * curvature
        vector = cosine * vector + sine * direction
        image = cosine * image + sine * applied
    row, col = iota((rows_a, 128), 0), iota((rows_a, 128), 1)
    for j in range(B * B // 128):
        kept = jnp.where((row & 31) == (col >> 5) + 4 * j, vector, 0.0)
        ground_ref[:, pl.ds(j * 128, 128)] = jnp.sum(kept.reshape(sec, B, 128), axis=1)
    energy_ref[...] = jnp.broadcast_to(energy, (8, 128))

    for k in range(1, n_sector):
        red_copy(DAV_ITERS, k, member).wait_send()


def local(
    env_in, mpo_terms, site_tensors, route_owner, route_sector, live_block_extent, psi, right_env
):
    n_sector = lax.axis_size("sector")
    n_site = lax.axis_size("site")
    member = lax.axis_index("sector")
    sec, bond = env_in.shape[0], env_in.shape[1]
    phys = site_tensors.shape[2]
    steps = n_site - 1
    n_high = n_sector // 2
    dr = B // n_site
    own = sec * dr
    cols = phys * own
    rows_a, wide = sec * B, bond * B
    cut = (wide // 128 + 1) // 2 * 128
    parts = ((0, cut), (cut, wide - cut))
    n_parts = len(parts)

    target = route_owner[0, :, :, 0] * sec + route_sector[0]
    target = lax.dynamic_slice_in_dim(target, member * sec, sec, 0)
    goals = jnp.broadcast_to(target.T[:, :, None], (phys, sec, dr)).reshape(cols // 128, 128)
    goals = jnp.pad(goals.astype(BF16), ((0, 16 - cols // 128), (0, 0)))
    extent = jnp.broadcast_to(live_block_extent.astype(F32)[:, None, None], (sec, B, 128)).reshape(rows_a, 128)

    count_all = float(sec * n_sector * B * B)
    dma = pltpu.SemaphoreType.DMA
    ground, energy = pl.pallas_call(
        functools.partial(kernel, n_site, n_sector, sec, phys, bond, count_all, parts),
        out_shape=(
            jax.ShapeDtypeStruct((sec, B * B), F32),
            jax.ShapeDtypeStruct((8, 128), F32),
        ),
        in_specs=[pl.BlockSpec(memory_space=pltpu.HBM if i < 2 else pltpu.VMEM) for i in range(7)],
        out_specs=[pl.BlockSpec(memory_space=pltpu.VMEM), pl.BlockSpec(memory_space=pltpu.VMEM)],
        scratch_shapes=[
            pltpu.VMEM((phys, wide, wide), BF16),
            pltpu.VMEM((n_site, rows_a + 16, 128), BF16),
            pltpu.VMEM((steps, n_sector * own, wide), BF16),
            pltpu.VMEM((steps, n_high, own, wide), BF16),
            pltpu.VMEM((steps, n_high, own, wide), BF16),
            pltpu.VMEM((steps, n_high, own, wide), BF16),
            pltpu.VMEM((steps, rows_a, wide), BF16),
            pltpu.VMEM((rows_a, wide), BF16),
            pltpu.VMEM((rows_a, wide), BF16),
            pltpu.VMEM((phys, rows_a, wide), BF16),
            pltpu.VMEM((cols, wide), BF16),
            pltpu.VMEM((sec, 128, phys * 128), BF16),
            pltpu.VMEM((cols, rows_a), BF16),
            pltpu.VMEM((n_sector * own, cols), BF16),
            pltpu.VMEM((DAV_ITERS + 1, n_sector, 8, 128), F32),
            pltpu.VMEM((DAV_ITERS + 1, 8, 128), F32),
            pltpu.VMEM((wide, rows_a), BF16),
            pltpu.VMEM((wide, rows_a), BF16),
            pltpu.VMEM((rows_a, wide), F32),
            pltpu.VMEM((bond, sec, B * B), F32),
            pltpu.VMEM((bond, sec, B * B), BF16),
            pltpu.VMEM((bond, sec, B * B), BF16),
            dma((n_site,)), dma((n_site,)),
            dma((steps, n_parts, n_high)), dma((steps, n_parts, n_high)),
            dma((steps, n_parts, n_high)), dma((steps, n_parts, n_high)),
            dma((steps, n_parts, n_site)), dma((steps, n_parts, n_site)),
            dma((DAV_ITERS + 1, n_sector)), dma((DAV_ITERS + 1, n_sector)),
            dma((2,)),
        ],
        compiler_params=pltpu.CompilerParams(
            collective_id=0, has_side_effects=True, vmem_limit_bytes=50 * 1024 * 1024
        ),
    )(env_in.transpose(1, 0, 2), right_env[0].transpose(1, 0, 2), site_tensors[0], psi[0], mpo_terms, goals, extent)
    return ground[None], energy[0, :1]


def solution(mesh):
    in_specs = (
        P("sector", None, None),
        P(),
        P("site", "sector", None, None),
        P("site", None, None, None),
        P("site", None, None),
        P("sector"),
        P("site", "sector", None),
        P("site", "sector", None, None),
    )
    out_specs = (P("site", "sector", None), P("site"))
    return jax.shard_map(local, mesh=mesh, in_specs=in_specs, out_specs=out_specs, check_vma=False)
```
